32 devices in a mesh: run: 2 (over y), tile: 8 (over z, x), depth: 2 (over core).
Axes of the slice: x: 2, y: 2, z: 4, core: 2. Of those that a mesh axis runs over, the one named last changes fastest.
Arguments:
- dissolved: bfloat16 [128, 16, 256], P(('run', 'tile', 'depth')), parts along dimension 0, may hold values from -6 to 6
- sorbed: bfloat16 [128, 16, 256], P(('run', 'tile', 'depth')), parts along dimension 0, may hold values from -6 to 6
- tf_table: float32 [4, 256], replicated, may hold values from 0.1 to 1
Outputs:
- gradient_norms: float32 [2, 128, 16, 256], P(None, ('run', 'tile', 'depth')), parts along dimension 1
- rendered: float32 [4, 32, 256], P(None, ('run', 'tile', 'depth')), parts along dimension 1
The draws below stay inside these ranges and needn't reach their ends.
There are 2 independent parts, one for each index of `run`. The reference program is written for one: setup_inputs(seed, part) draws one part's arguments, and reference() takes and returns one part's arrays. A program takes and returns all parts, laid end to end along the dimension named above; an argument that names none is the same for every part. Nothing has to cross between parts.
All inputs are finite; a program needn't handle non-finite values.
Results may differ from the reference program's by a relative error of at most 0.0003.
Values may be sent and summed in bfloat16 or wider, within the bound.
A program may use at most 320 MiB of HBM per device.

```python
import math
import jax
import jax.numpy as jnp
from jax import lax

CZ = 4
NY = 256
TF_ENTRIES = 256
NZ = 64
NX = 16


def steps_of(stream_key, dims, pieces, smallest, top_value):
    loudness, own = 1.0, jax.random.fold_in(stream_key, 6)
    for dim, blocks in pieces:
        steps = jnp.exp(jax.random.uniform(jax.random.fold_in(own, dim), (blocks,), jnp.float32, smallest / len(pieces), top_value / len(pieces)))
        loudness = loudness * jnp.repeat(steps, dims[dim] // blocks).reshape([-1 if axis == dim else 1 for axis in range(len(dims))])
    return loudness


def bell_draw(own_key, extent, spread, most, shards=(), kind=jnp.bfloat16):
    values = jax.random.normal(own_key, extent, jnp.float32) * spread
    if len(shards) > 0:
        values = steps_of(own_key, extent, shards, -0.22, 0.18) * values
    return jnp.clip(values, min=-most, max=most).astype(kind)


def setup_inputs(seed: int = 0, part: int = 0) -> dict:
    key_of = jax.random.split(jax.random.key(seed), 4)
    part_splits = jax.random.split(jax.random.fold_in(key_of[3], part), 4)
    dissolved = bell_draw(part_splits[0], (NZ, NX, NY), 1.0, 6.0, ((0, 16),))
    sorbed = bell_draw(part_splits[1], (NZ, NX, NY), 1.0, 6.0, ((0, 16),))
    tf_table = jnp.clip(jax.random.uniform(key_of[2], (4, TF_ENTRIES), jnp.float32, 0.1, 1.0), 0.1, 1.0)
    return {"dissolved": dissolved, "sorbed": sorbed, "tf_table": tf_table}


spread_cells = 1.5
cell_spacing = 0.05
bell_values = [math.exp(-(offset * offset) / (2.0 * spread_cells * spread_cells)) for offset in range(-3, 4)]
gauss_taps = [value / sum(bell_values) for value in bell_values]
slope_norm = sum(((offset - 3) * (offset - 3) * bell_values[offset] for offset in range(7)))
slope_taps = [(offset - 3) * bell_values[offset] / slope_norm / cell_spacing for offset in range(7)]
light_vector = (0.48, 0.6, 0.64)

def apply_taps(source, along_dim, weights, length):
    summed = weights[0] * lax.slice_in_dim(source, 0, length, axis=along_dim)
    for offset in range(1, 7):
        summed = summed + weights[offset] * lax.slice_in_dim(source, offset, offset + length, axis=along_dim)
    return summed

def band_matrix(length, weights):
    row_ids = lax.broadcasted_iota(jnp.int32, (length, length), 0)
    col_ids = lax.broadcasted_iota(jnp.int32, (length, length), 1)
    offsets = col_ids - row_ids
    matrix = jnp.zeros((length, length), jnp.float32)
    for offset in range(7):
        matrix = matrix + jnp.where(offsets == offset - 3, weights[offset], 0.0)
    return matrix

def filter_rows(source, matrix):
    return jnp.einsum('fzxy,wx->fzwy', source, matrix, precision=lax.Precision.HIGHEST)

def filter_columns(source, matrix):
    return jnp.einsum('fzxy,wy->fzxw', source, matrix, precision=lax.Precision.HIGHEST)

def shade_cells(window, table, z_first, total_depth):
    depth_cells = window.shape[1] - 6
    fields = window.astype(jnp.float32)
    rows = fields.shape[2]
    columns = fields.shape[3]
    gauss_rows = band_matrix(rows, gauss_taps)
    slope_rows = band_matrix(rows, slope_taps)
    gauss_cols = band_matrix(columns, gauss_taps)
    slope_cols = band_matrix(columns, slope_taps)
    smooth_z = apply_taps(fields, 1, gauss_taps, depth_cells)
    slope_z = apply_taps(fields, 1, slope_taps, depth_cells)
    smooth_zx = filter_rows(smooth_z, gauss_rows)
    grad_x = filter_columns(filter_rows(smooth_z, slope_rows), gauss_cols)
    grad_y = filter_columns(smooth_zx, slope_cols)
    grad_z = filter_columns(filter_rows(slope_z, gauss_rows), gauss_cols)
    squared = grad_x * grad_x + grad_y * grad_y + grad_z * grad_z
    grad_norms = jnp.sqrt(squared)
    concentration = fields[0, 3:3 + depth_cells]
    entries = table.shape[1]
    position = jax.nn.sigmoid(concentration) * (entries - 1)
    lower_idx = jnp.minimum(jnp.floor(position), entries - 2)
    weight_hi = position - lower_idx
    index_low = lower_idx.astype(jnp.int32)
    lower_entry = jnp.take(table, index_low, axis=1)
    upper_entry = jnp.take(table, index_low + 1, axis=1)
    looked = lower_entry + weight_hi[None] * (upper_entry - lower_entry)
    facing = light_vector[0] * grad_z[0] + light_vector[1] * grad_x[0] + light_vector[2] * grad_y[0]
    shading = 0.25 + 0.75 * jnp.abs(facing) / jnp.sqrt(1.0 + squared[0])
    heights = (z_first + jnp.arange(depth_cells, dtype=jnp.int32)).astype(jnp.float32)
    depth_cue = 1.0 - 0.5 * (heights + 0.5) / total_depth
    sorb_term = squared[1] / (1.0 + squared[1])
    extinct = 3.0 / total_depth * looked[3] * (1.0 + sorb_term)
    opacity = -jnp.expm1(-extinct)
    colors = looked[:3] * (shading * depth_cue[:, None, None] * opacity)[None]
    return (grad_norms, colors, extinct)

def reference(dissolved, sorbed, tf_table):
    bricks = jnp.stack([dissolved, sorbed])
    padded = jnp.pad(bricks, ((0, 0), (3, 3), (0, 0), (0, 0)))
    block_cells = CZ * 8
    block_count = NZ // block_cells

    def render_block(carried, block_index):
        color_sum, depth_sum = carried
        start = (block_index * block_cells).astype(jnp.int32)
        window = lax.dynamic_slice_in_dim(padded, start, block_cells + 6, axis=1)
        grad_norms, colors, extinct = shade_cells(window, tf_table, start, NZ)
        prefix = jnp.cumsum(extinct, axis=0) - extinct
        emitted = lax.optimization_barrier(jnp.sum(colors * jnp.exp(-prefix)[None], axis=1))
        color_sum = color_sum + jnp.exp(-depth_sum)[None] * emitted
        depth_sum = depth_sum + lax.optimization_barrier(jnp.sum(extinct, axis=0))
        return ((color_sum, depth_sum), grad_norms)
    start_state = (jnp.zeros((3, NX, NY), jnp.float32), jnp.zeros((NX, NY), jnp.float32))
    final_state, stacked = lax.scan(render_block, start_state, jnp.arange(block_count, dtype=jnp.int32))
    color_sum, depth_sum = final_state
    grad_all = jnp.transpose(stacked, (1, 0, 2, 3, 4)).reshape(2, NZ, NX, NY)
    rendered = jnp.concatenate([color_sum, (1.0 - jnp.exp(-depth_sum))[None]], axis=0)
    return (grad_all, rendered)
```

```python
import functools
import math

import jax
import jax.numpy as jnp
from jax import lax
from jax.experimental import pallas as pl
from jax.experimental.pallas import tpu as pltpu
from jax.sharding import PartitionSpec as P

MESH = pl.DeviceIdType.MESH
REACH = 3
SPREAD = 4.5
ROWS = 16
LANES = 128
BELL = [math.exp(-(k * k) / SPREAD) for k in range(-REACH, REACH + 1)]
SMOOTH = 1.0 / sum(BELL)
SLOPE = 20.0 / sum(k * k * BELL[k + REACH] for k in range(-REACH, REACH + 1))
LIGHT = (0.48, 0.6, 0.64)


def two_parts(values):
    high = values.astype(jnp.bfloat16)
    low = (values - high.astype(jnp.float32)).astype(jnp.bfloat16)
    return high, low


def plane_weights(weights_ref, depth, window, shift):
    cells = depth * ROWS
    shape = (cells, (depth + 2 * REACH) * window)
    row = lax.broadcasted_iota(jnp.int32, shape, 0)
    col = lax.broadcasted_iota(jnp.int32, shape, 1)
    dz = col // window - row // ROWS - REACH
    dx = col % window - row % ROWS - shift
    near = (jnp.abs(dz) <= REACH) & (jnp.abs(dx) <= REACH)
    dz = dz.astype(jnp.float32)
    dx = dx.astype(jnp.float32)
    bell = jnp.where(near, jnp.exp((dz * dz + dx * dx) * (-1.0 / SPREAD)), 0.0)
    parts = (
        bell * dz * (SLOPE * SMOOTH),
        bell * dx * (SLOPE * SMOOTH),
        bell * (SMOOTH * SMOOTH),
    )
    for k, part in enumerate(parts):
        high, low = two_parts(part)
        weights_ref[pl.ds(k * cells, cells), :] = high
        weights_ref[pl.ds((k + 3) * cells, cells), :] = low


def line_weights(lines_ref, columns):
    shape = (columns, columns)
    offset = lax.broadcasted_iota(jnp.int32, shape, 0) - lax.broadcasted_iota(jnp.int32, shape, 1)
    near = jnp.abs(offset) <= REACH
    offset = offset.astype(jnp.float32)
    bell = jnp.where(near, jnp.exp(offset * offset * (-1.0 / SPREAD)), 0.0)
    lines_ref[0], lines_ref[1] = two_parts(bell * SMOOTH)
    lines_ref[2], lines_ref[3] = two_parts(bell * offset * SLOPE)


def matmul(a, b):
    return jnp.dot(a, b, preferred_element_type=jnp.float32)


def lookup(table, step, position):
    lower = jnp.minimum(jnp.floor(position), table.shape[1] - 2.0)
    fraction = position - lower
    index = lower.astype(jnp.int32)
    lane = index % LANES
    group = index // LANES
    values = []
    for c in range(4):
        base = None
        for g in range(table.shape[1] // LANES):
            pair = []
            for source in (table, step):
                entries = jnp.broadcast_to(
                    source[c : c + 1, g * LANES : (g + 1) * LANES], position.shape
                )
                pair.append(
                    jnp.take_along_axis(entries, lane, axis=1, mode="promise_in_bounds")
                )
            if base is None:
                base, slope = pair
            else:
                base = jnp.where(group == g, pair[0], base)
                slope = jnp.where(group == g, pair[1], slope)
        values.append(base + fraction * slope)
    return values


def kernel(
    tiles, depths, dissolved, sorbed, table_ref, norms, rendered,
    cells, weights, lines, looked, send, recv,
    halo_send, halo_recv, image_send, image_recv,
):
    depth, rows, columns = dissolved.shape
    group = tiles * depths
    total = depth * group
    chunks = rows // ROWS
    shift = 0 if chunks == 1 else ROWS
    window = ROWS + 2 * shift
    halves = columns // LANES
    run = lax.axis_index("run")
    me = lax.axis_index("tile") * depths + lax.axis_index("depth")

    def device(slab):
        return (run, slab // depths, slab % depths)

    def peers(body):
        if group <= 32:
            for k in range(1, group):
                body(lax.rem(me + k, group))
        else:
            @pl.loop(1, group)
            def _(k):
                body(lax.rem(me + k, group))

    barrier = pltpu.get_barrier_semaphore()
    peers(lambda p: pl.semaphore_signal(barrier, inc=1, device_id=device(p), device_id_type=MESH))
    pl.semaphore_wait(barrier, group - 1)

    inner = pl.ds(shift, rows)

    def halo(field, up):
        source = (dissolved, sorbed)[field]
        k = 2 * field + up
        return pltpu.make_async_remote_copy(
            src_ref=source.at[pl.ds(depth - REACH, REACH)] if up else source.at[pl.ds(0, REACH)],
            dst_ref=cells.at[field, pl.ds(0 if up else depth + REACH, REACH), inner],
            send_sem=halo_send.at[k],
            recv_sem=halo_recv.at[k],
            device_id=device(me + 1 if up else me - 1),
            device_id_type=MESH,
        )

    first, last = me == 0, me == group - 1

    @pl.when(jnp.logical_not(last))
    def _():
        for field in range(2):
            halo(field, 1).start()

    @pl.when(jnp.logical_not(first))
    def _():
        for field in range(2):
            halo(field, 0).start()

    @pl.when(first)
    def _():
        for field in range(2):
            cells[field, pl.ds(0, REACH), inner] = jnp.zeros((REACH, rows, columns), jnp.bfloat16)

    @pl.when(last)
    def _():
        for field in range(2):
            cells[field, pl.ds(depth + REACH, REACH), inner] = jnp.zeros(
                (REACH, rows, columns), jnp.bfloat16
            )

    if shift:
        edge = jnp.zeros((depth + 2 * REACH, shift, columns), jnp.bfloat16)
        for field in range(2):
            cells[field, :, pl.ds(0, shift)] = edge
            cells[field, :, pl.ds(shift + rows, shift)] = edge
    cells[0, pl.ds(REACH, depth), inner] = dissolved[...]
    cells[1, pl.ds(REACH, depth), inner] = sorbed[...]

    plane_weights(weights, depth, window, shift)
    line_weights(lines, columns)

    table = table_ref[...]
    step = pltpu.roll(table, table.shape[1] - 1, 1) - table

    def look(x0):
        for z in range(depth):
            level = dissolved[z, pl.ds(x0, ROWS), :].astype(jnp.float32)
            position = (table.shape[1] - 1.0) / (1.0 + jnp.exp(-level))
            for h in range(halves):
                span = slice(h * LANES, (h + 1) * LANES)
                for r in range(0, ROWS, 8):
                    found = lookup(table, step, position[r : r + 8, span])
                    for c in range(4):
                        looked[c, z, pl.ds(r, 8), span] = found[c]

    def shade(x0):
        plane = depth * ROWS
        flat = []
        for field in range(2):
            piece = cells[field, :, pl.ds(x0, window), :].reshape(-1, columns)
            both = matmul(weights[...], piece)
            flat.append(both[: 3 * plane] + both[3 * plane :])
        smooth_in = jnp.concatenate([flat[0][: 2 * plane], flat[1][: 2 * plane]], axis=0)
        slope_in = jnp.concatenate([flat[0][2 * plane :], flat[1][2 * plane :]], axis=0)
        high, low = two_parts(smooth_in)
        smoothed = matmul(high, lines[0]) + matmul(low, lines[0]) + matmul(high, lines[1])
        high, low = two_parts(slope_in)
        sloped = matmul(high, lines[2]) + matmul(low, lines[2]) + matmul(high, lines[3])

        emitted = [None] * 3
        transmit = None
        for z in range(depth):
            here = slice(z * ROWS, (z + 1) * ROWS)
            squares = []
            for field in range(2):
                gz = smoothed[2 * field * plane :][here]
                gx = smoothed[(2 * field + 1) * plane :][here]
                gy = sloped[field * plane :][here]
                square = gx * gx + gy * gy + gz * gz
                norms[field, z, pl.ds(x0, ROWS), :] = jnp.sqrt(square)
                squares.append(square)
                if field == 0:
                    facing = LIGHT[0] * gz + LIGHT[1] * gx + LIGHT[2] * gy
            shading = 0.25 + 0.75 * jnp.abs(facing) * lax.rsqrt(1.0 + squares[0])
            height = (me * depth + z).astype(jnp.float32)
            cue = 1.0 - (height + 0.5) * (0.5 / total)
            extinct = (3.0 / total) * looked[3, z] * (2.0 - 1.0 / (1.0 + squares[1]))
            passing = jnp.exp(-extinct)
            strength = shading * cue * (1.0 - passing)
            if z:
                strength = strength * transmit
            for c in range(3):
                colour = looked[c, z] * strength
                emitted[c] = colour if z == 0 else emitted[c] + colour
            transmit = passing if z == 0 else transmit * passing
        for c, layer in enumerate(emitted + [transmit]):
            for h in range(halves):
                send[pl.ds(x0, ROWS), c * halves + h, :] = layer[:, h * LANES : (h + 1) * LANES]

    def arrive():
        @pl.when(jnp.logical_not(first))
        def _():
            for field in range(2):
                halo(field, 1).wait_recv()

        @pl.when(jnp.logical_not(last))
        def _():
            for field in range(2):
                halo(field, 0).wait_recv()

    if chunks == 1:
        look(0)
        arrive()
        shade(0)
    else:
        arrive()

        @pl.loop(0, chunks)
        def _(chunk):
            x0 = pl.multiple_of(chunk * ROWS, ROWS)
            look(x0)
            shade(x0)

    def image(slab):
        return pltpu.make_async_remote_copy(
            src_ref=send.at[slab],
            dst_ref=recv.at[me],
            send_sem=image_send,
            recv_sem=image_recv,
            device_id=device(slab),
            device_id_type=MESH,
        )

    peers(lambda p: image(p).start())
    recv[me] = send[me]

    others = pltpu.make_async_remote_copy(
        src_ref=send.at[pl.ds(0, group - 1)],
        dst_ref=recv.at[pl.ds(0, group - 1)],
        send_sem=image_send,
        recv_sem=image_recv,
        device_id=device(lax.rem(me + 1, group)),
        device_id_type=MESH,
    )
    others.wait_recv()

    order = lax.broadcasted_iota(jnp.int32, (group, LANES), 0)
    for h in range(halves):
        span = slice(h * LANES, (h + 1) * LANES)
        through = recv[:, 3 * halves + h, :]
        hop = 1
        while hop < group:
            through = through * jnp.where(order >= hop, pltpu.roll(through, hop, 0), 1.0)
            hop *= 2
        ahead = jnp.where(order >= 1, pltpu.roll(through, 1, 0), 1.0)
        for c in range(3):
            rendered[c, :, span] = jnp.sum(
                recv[:, c * halves + h, :] * ahead, axis=0, keepdims=True
            )
        rendered[3, :, span] = 1.0 - through[group - 1 :]

    @pl.when(jnp.logical_not(last))
    def _():
        for field in range(2):
            halo(field, 1).wait_send()

    @pl.when(jnp.logical_not(first))
    def _():
        for field in range(2):
            halo(field, 0).wait_send()

    others.wait_send()


def local(tiles, depths, dissolved, sorbed, table):
    depth, rows, columns = dissolved.shape
    group = tiles * depths
    assert rows == group and rows % ROWS == 0 and columns % LANES == 0 and depth >= REACH
    shift = 0 if rows == ROWS else ROWS
    halves = columns // LANES
    padded = depth + 2 * REACH
    return pl.pallas_call(
        functools.partial(kernel, tiles, depths),
        out_shape=(
            jax.ShapeDtypeStruct((2, depth, rows, columns), jnp.float32),
            jax.ShapeDtypeStruct((4, rows // group, columns), jnp.float32),
        ),
        in_specs=[pl.BlockSpec(memory_space=pltpu.VMEM)] * 3,
        out_specs=(pl.BlockSpec(memory_space=pltpu.VMEM),) * 2,
        scratch_shapes=[
            pltpu.VMEM((2, padded, rows + 2 * shift, columns), jnp.bfloat16),
            pltpu.VMEM((6 * depth * ROWS, padded * (ROWS + 2 * shift)), jnp.bfloat16),
            pltpu.VMEM((4, columns, columns), jnp.bfloat16),
            pltpu.VMEM((4, depth, ROWS, columns), jnp.float32),
            pltpu.VMEM((group, 4 * halves, LANES), jnp.float32),
            pltpu.VMEM((group, 4 * halves, LANES), jnp.float32),
            pltpu.SemaphoreType.DMA((4,)),
            pltpu.SemaphoreType.DMA((4,)),
            pltpu.SemaphoreType.DMA,
            pltpu.SemaphoreType.DMA,
        ],
        compiler_params=pltpu.CompilerParams(
            collective_id=0, has_side_effects=True, vmem_limit_bytes=32 * 1024 * 1024
        ),
    )(dissolved, sorbed, table)


def solution(mesh):
    return jax.shard_map(
        functools.partial(local, mesh.shape["tile"], mesh.shape["depth"]),
        mesh=mesh,
        in_specs=(
            P(("run", "tile", "depth"), None, None),
            P(("run", "tile", "depth"), None, None),
            P(),
        ),
        out_specs=(
            P(None, ("run", "tile", "depth"), None, None),
            P(None, ("run", "tile", "depth"), None),
        ),
        check_vma=False,
    )
```

```python
import functools
import math

import jax
import jax.numpy as jnp
from jax import lax
from jax.experimental import pallas as pl
from jax.experimental.pallas import tpu as pltpu
from jax.sharding import PartitionSpec as P

MESH = pl.DeviceIdType.MESH
REACH = 3
SPREAD = 4.5
ROWS = 16
LANES = 128
BELL = [math.exp(-(k * k) / SPREAD) for k in range(-REACH, REACH + 1)]
SMOOTH = 1.0 / sum(BELL)
SLOPE = 20.0 / sum(k * k * BELL[k + REACH] for k in range(-REACH, REACH + 1))
LIGHT = (0.48, 0.6, 0.64)


def two_parts(values):
    high = values.astype(jnp.bfloat16)
    low = (values - high.astype(jnp.float32)).astype(jnp.bfloat16)
    return high, low


def plane_weights(weights_ref, depth, window, shift):
    cells = depth * ROWS
    shape = (cells, (depth + 2 * REACH) * window)
    row = lax.broadcasted_iota(jnp.int32, shape, 0)
    col = lax.broadcasted_iota(jnp.int32, shape, 1)
    dz = col // window - row // ROWS - REACH
    dx = col % window - row % ROWS - shift
    near = (jnp.abs(dz) <= REACH) & (jnp.abs(dx) <= REACH)
    dz = dz.astype(jnp.float32)
    dx = dx.astype(jnp.float32)
    bell = jnp.where(near, jnp.exp((dz * dz + dx * dx) * (-1.0 / SPREAD)), 0.0)
    parts = (
        bell * dz * (SLOPE * SMOOTH),
        bell * dx * (SLOPE * SMOOTH),
        bell * (SMOOTH * SMOOTH),
    )
    for k, part in enumerate(parts):
        high, low = two_parts(part)
        weights_ref[pl.ds(k * cells, cells), :] = high
        weights_ref[pl.ds((k + 3) * cells, cells), :] = low


def line_weights(lines_ref, columns):
    shape = (columns, columns)
    offset = lax.broadcasted_iota(jnp.int32, shape, 0) - lax.broadcasted_iota(jnp.int32, shape, 1)
    near = jnp.abs(offset) <= REACH
    offset = offset.astype(jnp.float32)
    bell = jnp.where(near, jnp.exp(offset * offset * (-1.0 / SPREAD)), 0.0)
    lines_ref[0], lines_ref[1] = two_parts(bell * SMOOTH)
    lines_ref[2], lines_ref[3] = two_parts(bell * offset * SLOPE)


def matmul(a, b):
    return jnp.dot(a, b, preferred_element_type=jnp.float32)


def lookup(table, step, position):
    lower = jnp.minimum(jnp.floor(position), table.shape[1] - 2.0)
    fraction = position - lower
    index = lower.astype(jnp.int32)
    lane = index % LANES
    group = index // LANES
    values = []
    for c in range(4):
        base = None
        for g in range(table.shape[1] // LANES):
            pair = []
            for source in (table, step):
                entries = jnp.broadcast_to(
                    source[c : c + 1, g * LANES : (g + 1) * LANES], position.shape
                )
                pair.append(
                    jnp.take_along_axis(entries, lane, axis=1, mode="promise_in_bounds")
                )
            if base is None:
                base, slope = pair
            else:
                base = jnp.where(group == g, pair[0], base)
                slope = jnp.where(group == g, pair[1], slope)
        values.append(base + fraction * slope)
    return values


def kernel(
    tiles, depths, dissolved, sorbed, table_in, norms, recv,
    cells, table_ref, weights, lines, looked, send,
    load_sem, halo_send, halo_recv, image_send, image_recv,
):
    depth, rows, columns = dissolved.shape
    group = tiles * depths
    total = depth * group
    chunks = rows // ROWS
    shift = 0 if chunks == 1 else ROWS
    window = ROWS + 2 * shift
    halves = columns // LANES
    run = lax.axis_index("run")
    me = lax.axis_index("tile") * depths + lax.axis_index("depth")
    inner = pl.ds(shift, rows)

    def device(slab):
        return (run, slab // depths, slab % depths)

    def peers(body):
        if group <= 32:
            for k in range(1, group):
                body(lax.rem(me + k, group))
        else:
            @pl.loop(1, group)
            def _(k):
                body(lax.rem(me + k, group))

    barrier = pltpu.get_barrier_semaphore()
    peers(lambda p: pl.semaphore_signal(barrier, inc=1, device_id=device(p), device_id_type=MESH))

    loads = [
        pltpu.make_async_copy(dissolved, cells.at[0, pl.ds(REACH, depth), inner], load_sem.at[0]),
        pltpu.make_async_copy(table_in, table_ref, load_sem.at[1]),
        pltpu.make_async_copy(sorbed, cells.at[1, pl.ds(REACH, depth), inner], load_sem.at[2]),
    ]
    for load in loads:
        load.start()

    first, last = me == 0, me == group - 1

    @pl.when(first)
    def _():
        for field in range(2):
            cells[field, pl.ds(0, REACH), inner] = jnp.zeros((REACH, rows, columns), jnp.bfloat16)

    @pl.when(last)
    def _():
        for field in range(2):
            cells[field, pl.ds(depth + REACH, REACH), inner] = jnp.zeros(
                (REACH, rows, columns), jnp.bfloat16
            )

    if shift:
        edge = jnp.zeros((depth + 2 * REACH, shift, columns), jnp.bfloat16)
        for field in range(2):
            cells[field, :, pl.ds(0, shift)] = edge
            cells[field, :, pl.ds(shift + rows, shift)] = edge

    plane_weights(weights, depth, window, shift)

    pl.semaphore_wait(barrier, group - 1)

    def halo(field, up):
        source = (dissolved, sorbed)[field]
        k = 2 * field + up
        return pltpu.make_async_remote_copy(
            src_ref=source.at[pl.ds(depth - REACH, REACH)] if up else source.at[pl.ds(0, REACH)],
            dst_ref=cells.at[field, pl.ds(0 if up else depth + REACH, REACH), inner],
            send_sem=halo_send.at[k],
            recv_sem=halo_recv.at[k],
            device_id=device(me + 1 if up else me - 1),
            device_id_type=MESH,
        )

    @pl.when(jnp.logical_not(last))
    def _():
        for field in range(2):
            halo(field, 1).start()

    @pl.when(jnp.logical_not(first))
    def _():
        for field in range(2):
            halo(field, 0).start()

    line_weights(lines, columns)
    for load in loads:
        load.wait()

    table = table_ref[...]
    step = pltpu.roll(table, table.shape[1] - 1, 1) - table

    def look(x0):
        for z in range(depth):
            level = cells[0, REACH + z, pl.ds(shift + x0, ROWS), :].astype(jnp.float32)
            position = (table.shape[1] - 1.0) / (1.0 + jnp.exp(-level))
            for h in range(halves):
                span = slice(h * LANES, (h + 1) * LANES)
                for r in range(0, ROWS, 8):
                    found = lookup(table, step, position[r : r + 8, span])
                    for c in range(4):
                        looked[c, z, pl.ds(r, 8), span] = found[c]

    def shade(x0):
        plane = depth * ROWS
        flat = []
        for field in range(2):
            piece = cells[field, :, pl.ds(x0, window), :].reshape(-1, columns)
            both = matmul(weights[...], piece)
            flat.append(both[: 3 * plane] + both[3 * plane :])
        smooth_in = jnp.concatenate([flat[0][: 2 * plane], flat[1][: 2 * plane]], axis=0)
        slope_in = jnp.concatenate([flat[0][2 * plane :], flat[1][2 * plane :]], axis=0)
        high, low = two_parts(smooth_in)
        smoothed = matmul(high, lines[0]) + matmul(low, lines[0]) + matmul(high, lines[1])
        high, low = two_parts(slope_in)
        sloped = matmul(high, lines[2]) + matmul(low, lines[2]) + matmul(high, lines[3])

        emitted = [None] * 3
        transmit = None
        for z in range(depth):
            here = slice(z * ROWS, (z + 1) * ROWS)
            squares = []
            for field in range(2):
                gz = smoothed[2 * field * plane :][here]
                gx = smoothed[(2 * field + 1) * plane :][here]
                gy = sloped[field * plane :][here]
                square = gx * gx + gy * gy + gz * gz
                norms[field, z, pl.ds(x0, ROWS), :] = jnp.sqrt(square)
                squares.append(square)
                if field == 0:
                    facing = LIGHT[0] * gz + LIGHT[1] * gx + LIGHT[2] * gy
            shading = 0.25 + 0.75 * jnp.abs(facing) * lax.rsqrt(1.0 + squares[0])
            height = (me * depth + z).astype(jnp.float32)
            cue = 1.0 - (height + 0.5) * (0.5 / total)
            extinct = (3.0 / total) * looked[3, z] * (2.0 - 1.0 / (1.0 + squares[1]))
            passing = jnp.exp(-extinct)
            strength = shading * cue * (1.0 - passing)
            if z:
                strength = strength * transmit
            for c in range(3):
                colour = looked[c, z] * strength
                emitted[c] = colour if z == 0 else emitted[c] + colour
            transmit = passing if z == 0 else transmit * passing
        for c, layer in enumerate(emitted + [transmit]):
            for h in range(halves):
                send[pl.ds(x0, ROWS), c * halves + h, :] = layer[:, h * LANES : (h + 1) * LANES]

    def arrive():
        @pl.when(jnp.logical_not(first))
        def _():
            for field in range(2):
                halo(field, 1).wait_recv()

        @pl.when(jnp.logical_not(last))
        def _():
            for field in range(2):
                halo(field, 0).wait_recv()

    if chunks == 1:
        look(0)
        arrive()
        shade(0)
    else:
        arrive()

        @pl.loop(0, chunks)
        def _(chunk):
            x0 = pl.multiple_of(chunk * ROWS, ROWS)
            look(x0)
            shade(x0)

    def image(slab):
        return pltpu.make_async_remote_copy(
            src_ref=send.at[slab],
            dst_ref=recv.at[me],
            send_sem=image_send,
            recv_sem=image_recv,
            device_id=device(slab),
            device_id_type=MESH,
        )

    peers(lambda p: image(p).start())
    recv[me] = send[me]

    @pl.when(jnp.logical_not(last))
    def _():
        for field in range(2):
            halo(field, 1).wait_send()

    @pl.when(jnp.logical_not(first))
    def _():
        for field in range(2):
            halo(field, 0).wait_send()

    others = pltpu.make_async_remote_copy(
        src_ref=send.at[pl.ds(0, group - 1)],
        dst_ref=recv.at[pl.ds(0, group - 1)],
        send_sem=image_send,
        recv_sem=image_recv,
        device_id=device(lax.rem(me + 1, group)),
        device_id_type=MESH,
    )
    others.wait_send()
    others.wait_recv()


def finish(norms_in, pieces, norms_out, rendered_out, rendered, sem):
    group, parts, _ = pieces.shape
    halves = parts // 4
    norms_copy = pltpu.make_async_copy(norms_in, norms_out, sem.at[0])
    norms_copy.start()
    order = lax.broadcasted_iota(jnp.int32, (group, LANES), 0)
    for h in range(halves):
        span = slice(h * LANES, (h + 1) * LANES)
        through = pieces[:, 3 * halves + h, :]
        hop = 1
        while hop < group:
            through = through * jnp.where(order >= hop, pltpu.roll(through, hop, 0), 1.0)
            hop *= 2
        ahead = jnp.where(order >= 1, pltpu.roll(through, 1, 0), 1.0)
        for c in range(3):
            rendered[c, :, span] = jnp.sum(
                pieces[:, c * halves + h, :] * ahead, axis=0, keepdims=True
            )
        rendered[3, :, span] = 1.0 - through[group - 1 :]
    rendered_copy = pltpu.make_async_copy(rendered, rendered_out, sem.at[1])
    rendered_copy.start()
    norms_copy.wait()
    rendered_copy.wait()


def local(tiles, depths, dissolved, sorbed, table):
    depth, rows, columns = dissolved.shape
    group = tiles * depths
    assert rows == group and rows % ROWS == 0 and columns % LANES == 0 and depth >= REACH
    shift = 0 if rows == ROWS else ROWS
    halves = columns // LANES
    padded = depth + 2 * REACH
    norms, pieces = pl.pallas_call(
        functools.partial(kernel, tiles, depths),
        out_shape=(
            jax.ShapeDtypeStruct((2, depth, rows, columns), jnp.float32),
            jax.ShapeDtypeStruct((group, 4 * halves, LANES), jnp.float32),
        ),
        in_specs=[pl.BlockSpec(memory_space=pltpu.HBM)] * 3,
        out_specs=(pl.BlockSpec(memory_space=pltpu.VMEM),) * 2,
        scratch_shapes=[
            pltpu.VMEM((2, padded, rows + 2 * shift, columns), jnp.bfloat16),
            pltpu.VMEM(table.shape, jnp.float32),
            pltpu.VMEM((6 * depth * ROWS, padded * (ROWS + 2 * shift)), jnp.bfloat16),
            pltpu.VMEM((4, columns, columns), jnp.bfloat16),
            pltpu.VMEM((4, depth, ROWS, columns), jnp.float32),
            pltpu.VMEM((group, 4 * halves, LANES), jnp.float32),
            pltpu.SemaphoreType.DMA((3,)),
            pltpu.SemaphoreType.DMA((4,)),
            pltpu.SemaphoreType.DMA((4,)),
            pltpu.SemaphoreType.DMA,
            pltpu.SemaphoreType.DMA,
        ],
        compiler_params=pltpu.CompilerParams(
            collective_id=0, has_side_effects=True, vmem_limit_bytes=32 * 1024 * 1024
        ),
    )(dissolved, sorbed, table)
    return pl.pallas_call(
        finish,
        out_shape=(
            jax.ShapeDtypeStruct((2, depth, rows, columns), jnp.float32),
            jax.ShapeDtypeStruct((4, rows // group, columns), jnp.float32),
        ),
        in_specs=[pl.BlockSpec(memory_space=pltpu.VMEM)] * 2,
        out_specs=(pl.BlockSpec(memory_space=pltpu.HBM),) * 2,
        scratch_shapes=[
            pltpu.VMEM((4, rows // group, columns), jnp.float32),
            pltpu.SemaphoreType.DMA((2,)),
        ],
        compiler_params=pltpu.CompilerParams(vmem_limit_bytes=16 * 1024 * 1024),
    )(norms, pieces)


def solution(mesh):
    return jax.shard_map(
        functools.partial(local, mesh.shape["tile"], mesh.shape["depth"]),
        mesh=mesh,
        in_specs=(
            P(("run", "tile", "depth"), None, None),
            P(("run", "tile", "depth"), None, None),
            P(),
        ),
        out_specs=(
            P(None, ("run", "tile", "depth"), None, None),
            P(None, ("run", "tile", "depth"), None),
        ),
        check_vma=False,
    )
```

```python
import functools
import math

import jax
import jax.numpy as jnp
from jax import lax
from jax.experimental import pallas as pl
from jax.experimental.pallas import tpu as pltpu
from jax.sharding import PartitionSpec as P

MESH = pl.DeviceIdType.MESH
REACH = 3
SPREAD = 4.5
ROWS = 16
LANES = 128
BELL = [math.exp(-(k * k) / SPREAD) for k in range(-REACH, REACH + 1)]
SMOOTH = 1.0 / sum(BELL)
SLOPE = 20.0 / sum(k * k * BELL[k + REACH] for k in range(-REACH, REACH + 1))
LIGHT = (0.48, 0.6, 0.64)


def two_parts(values):
    high = values.astype(jnp.bfloat16)
    low = (values - high.astype(jnp.float32)).astype(jnp.bfloat16)
    return high, low


def plane_weights(weights_ref, depth, window, shift):
    cells = depth * ROWS
    shape = (cells, (depth + 2 * REACH) * window)
    row = lax.broadcasted_iota(jnp.int32, shape, 0)
    col = lax.broadcasted_iota(jnp.int32, shape, 1)
    dz = col // window - row // ROWS - REACH
    dx = col % window - row % ROWS - shift
    near = (jnp.abs(dz) <= REACH) & (jnp.abs(dx) <= REACH)
    dz = dz.astype(jnp.float32)
    dx = dx.astype(jnp.float32)
    bell = jnp.where(near, jnp.exp((dz * dz + dx * dx) * (-1.0 / SPREAD)), 0.0)
    parts = (
        bell * dz * (SLOPE * SMOOTH),
        bell * dx * (SLOPE * SMOOTH),
        bell * (SMOOTH * SMOOTH),
    )
    for k, part in enumerate(parts):
        high, low = two_parts(part)
        weights_ref[pl.ds(k * cells, cells), :] = high
        weights_ref[pl.ds((k + 3) * cells, cells), :] = low


def line_weights(lines_ref, columns):
    shape = (columns, columns)
    offset = lax.broadcasted_iota(jnp.int32, shape, 0) - lax.broadcasted_iota(jnp.int32, shape, 1)
    near = jnp.abs(offset) <= REACH
    offset = offset.astype(jnp.float32)
    bell = jnp.where(near, jnp.exp(offset * offset * (-1.0 / SPREAD)), 0.0)
    lines_ref[0], lines_ref[1] = two_parts(bell * SMOOTH)
    lines_ref[2], lines_ref[3] = two_parts(bell * offset * SLOPE)


def matmul(a, b):
    return jnp.dot(a, b, preferred_element_type=jnp.float32)


def lookup(table, step, position):
    lower = jnp.minimum(jnp.floor(position), table.shape[1] - 2.0)
    fraction = position - lower
    index = lower.astype(jnp.int32)
    lane = index % LANES
    group = index // LANES
    values = []
    for c in range(4):
        base = None
        for g in range(table.shape[1] // LANES):
            pair = []
            for source in (table, step):
                entries = jnp.broadcast_to(
                    source[c : c + 1, g * LANES : (g + 1) * LANES], position.shape
                )
                pair.append(
                    jnp.take_along_axis(entries, lane, axis=1, mode="promise_in_bounds")
                )
            if base is None:
                base, slope = pair
            else:
                base = jnp.where(group == g, pair[0], base)
                slope = jnp.where(group == g, pair[1], slope)
        values.append(base + fraction * slope)
    return values


def kernel(
    tiles, depths, dissolved, sorbed, table_in, norms, recv,
    cells, table_ref, weights, lines, looked, send,
    load_sem, halo_send, halo_recv, image_send, image_recv,
):
    depth, rows, columns = dissolved.shape
    group = tiles * depths
    total = depth * group
    chunks = rows // ROWS
    shift = 0 if chunks == 1 else ROWS
    window = ROWS + 2 * shift
    halves = columns // LANES
    run = lax.axis_index("run")
    me = lax.axis_index("tile") * depths + lax.axis_index("depth")
    inner = pl.ds(shift, rows)

    def device(slab):
        return (run, slab // depths, slab % depths)

    def peers(body):
        if group <= 32:
            for k in range(1, group):
                body(lax.rem(me + k, group))
        else:
            @pl.loop(1, group)
            def _(k):
                body(lax.rem(me + k, group))

    barrier = pltpu.get_barrier_semaphore()
    peers(lambda p: pl.semaphore_signal(barrier, inc=1, device_id=device(p), device_id_type=MESH))

    loads = [
        pltpu.make_async_copy(dissolved, cells.at[0, pl.ds(REACH, depth), inner], load_sem.at[0]),
        pltpu.make_async_copy(table_in, table_ref, load_sem.at[1]),
        pltpu.make_async_copy(sorbed, cells.at[1, pl.ds(REACH, depth), inner], load_sem.at[2]),
    ]
    for load in loads:
        load.start()

    first, last = me == 0, me == group - 1

    @pl.when(first)
    def _():
        for field in range(2):
            cells[field, pl.ds(0, REACH), inner] = jnp.zeros((REACH, rows, columns), jnp.bfloat16)

    @pl.when(last)
    def _():
        for field in range(2):
            cells[field, pl.ds(depth + REACH, REACH), inner] = jnp.zeros(
                (REACH, rows, columns), jnp.bfloat16
            )

    if shift:
        edge = jnp.zeros((depth + 2 * REACH, shift, columns), jnp.bfloat16)
        for field in range(2):
            cells[field, :, pl.ds(0, shift)] = edge
            cells[field, :, pl.ds(shift + rows, shift)] = edge

    plane_weights(weights, depth, window, shift)

    pl.semaphore_wait(barrier, group - 1)

    def halo(field, up):
        source = (dissolved, sorbed)[field]
        k = 2 * field + up
        return pltpu.make_async_remote_copy(
            src_ref=source.at[pl.ds(depth - REACH, REACH)] if up else source.at[pl.ds(0, REACH)],
            dst_ref=cells.at[field, pl.ds(0 if up else depth + REACH, REACH), inner],
            send_sem=halo_send.at[k],
            recv_sem=halo_recv.at[k],
            device_id=device(me + 1 if up else me - 1),
            device_id_type=MESH,
        )

    @pl.when(jnp.logical_not(last))
    def _():
        for field in range(2):
            halo(field, 1).start()

    @pl.when(jnp.logical_not(first))
    def _():
        for field in range(2):
            halo(field, 0).start()

    line_weights(lines, columns)
    for load in loads:
        load.wait()

    table = table_ref[...]
    step = pltpu.roll(table, table.shape[1] - 1, 1) - table

    def look(x0):
        for z in range(depth):
            level = cells[0, REACH + z, pl.ds(shift + x0, ROWS), :].astype(jnp.float32)
            position = (table.shape[1] - 1.0) / (1.0 + jnp.exp(-level))
            for h in range(halves):
                span = slice(h * LANES, (h + 1) * LANES)
                for r in range(0, ROWS, 8):
                    found = lookup(table, step, position[r : r + 8, span])
                    for c in range(4):
                        looked[c, z, pl.ds(r, 8), span] = found[c]

    def shade(x0):
        plane = depth * ROWS
        flat = []
        for field in range(2):
            piece = cells[field, :, pl.ds(x0, window), :].reshape(-1, columns)
            both = matmul(weights[...], piece)
            flat.append(both[: 3 * plane] + both[3 * plane :])
        smooth_in = jnp.concatenate([flat[0][: 2 * plane], flat[1][: 2 * plane]], axis=0)
        slope_in = jnp.concatenate([flat[0][2 * plane :], flat[1][2 * plane :]], axis=0)
        high, low = two_parts(smooth_in)
        smoothed = matmul(high, lines[0]) + matmul(low, lines[0]) + matmul(high, lines[1])
        high, low = two_parts(slope_in)
        sloped = matmul(high, lines[2]) + matmul(low, lines[2]) + matmul(high, lines[3])

        emitted = [None] * 3
        transmit = None
        for z in range(depth):
            here = slice(z * ROWS, (z + 1) * ROWS)
            squares = []
            for field in range(2):
                gz = smoothed[2 * field * plane :][here]
                gx = smoothed[(2 * field + 1) * plane :][here]
                gy = sloped[field * plane :][here]
                square = gx * gx + gy * gy + gz * gz
                norms[field, z, pl.ds(x0, ROWS), :] = jnp.sqrt(square)
                squares.append(square)
                if field == 0:
                    facing = LIGHT[0] * gz + LIGHT[1] * gx + LIGHT[2] * gy
            shading = 0.25 + 0.75 * jnp.abs(facing) * lax.rsqrt(1.0 + squares[0])
            height = (me * depth + z).astype(jnp.float32)
            cue = 1.0 - (height + 0.5) * (0.5 / total)
            extinct = (3.0 / total) * looked[3, z] * (2.0 - 1.0 / (1.0 + squares[1]))
            passing = jnp.exp(-extinct)
            strength = shading * cue * (1.0 - passing)
            if z:
                strength = strength * transmit
            for c in range(3):
                colour = looked[c, z] * strength
                emitted[c] = colour if z == 0 else emitted[c] + colour
            transmit = passing if z == 0 else transmit * passing
        for c, layer in enumerate(emitted + [transmit]):
            for h in range(halves):
                send[pl.ds(x0, ROWS), c * halves + h, :] = layer[:, h * LANES : (h + 1) * LANES]

    def arrive():
        @pl.when(jnp.logical_not(first))
        def _():
            for field in range(2):
                halo(field, 1).wait_recv()

        @pl.when(jnp.logical_not(last))
        def _():
            for field in range(2):
                halo(field, 0).wait_recv()

    if chunks == 1:
        look(0)
        arrive()
        shade(0)
    else:
        arrive()

        @pl.loop(0, chunks)
        def _(chunk):
            x0 = pl.multiple_of(chunk * ROWS, ROWS)
            look(x0)
            shade(x0)

    def image(slab):
        return pltpu.make_async_remote_copy(
            src_ref=send.at[slab],
            dst_ref=recv.at[me],
            send_sem=image_send,
            recv_sem=image_recv,
            device_id=device(slab),
            device_id_type=MESH,
        )

    peers(lambda p: image(p).start())
    recv[me] = send[me]

    @pl.when(jnp.logical_not(last))
    def _():
        for field in range(2):
            halo(field, 1).wait_send()

    @pl.when(jnp.logical_not(first))
    def _():
        for field in range(2):
            halo(field, 0).wait_send()

    others = pltpu.make_async_remote_copy(
        src_ref=send.at[pl.ds(0, group - 1)],
        dst_ref=recv.at[pl.ds(0, group - 1)],
        send_sem=image_send,
        recv_sem=image_recv,
        device_id=device(lax.rem(me + 1, group)),
        device_id_type=MESH,
    )
    others.wait_send()
    others.wait_recv()


def finish(norms_in, pieces, norms_out, rendered_out, rendered, sem):
    group, parts, _ = pieces.shape
    halves = parts // 4
    norms_copy = pltpu.make_async_copy(norms_in, norms_out, sem.at[0])
    norms_copy.start()
    order = lax.broadcasted_iota(jnp.int32, (group, LANES), 0)
    for h in range(halves):
        span = slice(h * LANES, (h + 1) * LANES)
        through = pieces[:, 3 * halves + h, :]
        hop = 1
        while hop < group:
            through = through * jnp.where(order >= hop, pltpu.roll(through, hop, 0), 1.0)
            hop *= 2
        ahead = jnp.where(order >= 1, pltpu.roll(through, 1, 0), 1.0)
        for c in range(3):
            rendered[c, :, span] = jnp.sum(
                pieces[:, c * halves + h, :] * ahead, axis=0, keepdims=True
            )
        rendered[3, :, span] = 1.0 - through[group - 1 :]
    rendered_copy = pltpu.make_async_copy(rendered, rendered_out, sem.at[1])
    rendered_copy.start()
    norms_copy.wait()
    rendered_copy.wait()


def local(tiles, depths, dissolved, sorbed, table):
    dissolved, sorbed, table = (
        pltpu.with_memory_space_constraint(whole, pltpu.HBM) for whole in (dissolved, sorbed, table)
    )
    depth, rows, columns = dissolved.shape
    group = tiles * depths
    assert rows == group and rows % ROWS == 0 and columns % LANES == 0 and depth >= REACH
    shift = 0 if rows == ROWS else ROWS
    halves = columns // LANES
    padded = depth + 2 * REACH
    norms, pieces = pl.pallas_call(
        functools.partial(kernel, tiles, depths),
        out_shape=(
            jax.ShapeDtypeStruct((2, depth, rows, columns), jnp.float32),
            jax.ShapeDtypeStruct((group, 4 * halves, LANES), jnp.float32),
        ),
        in_specs=[pl.BlockSpec(memory_space=pltpu.HBM)] * 3,
        out_specs=(pl.BlockSpec(memory_space=pltpu.VMEM),) * 2,
        scratch_shapes=[
            pltpu.VMEM((2, padded, rows + 2 * shift, columns), jnp.bfloat16),
            pltpu.VMEM(table.shape, jnp.float32),
            pltpu.VMEM((6 * depth * ROWS, padded * (ROWS + 2 * shift)), jnp.bfloat16),
            pltpu.VMEM((4, columns, columns), jnp.bfloat16),
            pltpu.VMEM((4, depth, ROWS, columns), jnp.float32),
            pltpu.VMEM((group, 4 * halves, LANES), jnp.float32),
            pltpu.SemaphoreType.DMA((3,)),
            pltpu.SemaphoreType.DMA((4,)),
            pltpu.SemaphoreType.DMA((4,)),
            pltpu.SemaphoreType.DMA,
            pltpu.SemaphoreType.DMA,
        ],
        compiler_params=pltpu.CompilerParams(
            collective_id=0, has_side_effects=True, vmem_limit_bytes=32 * 1024 * 1024
        ),
    )(dissolved, sorbed, table)
    return pl.pallas_call(
        finish,
        out_shape=(
            jax.ShapeDtypeStruct((2, depth, rows, columns), jnp.float32),
            jax.ShapeDtypeStruct((4, rows // group, columns), jnp.float32),
        ),
        in_specs=[pl.BlockSpec(memory_space=pltpu.VMEM)] * 2,
        out_specs=(pl.BlockSpec(memory_space=pltpu.HBM),) * 2,
        scratch_shapes=[
            pltpu.VMEM((4, rows // group, columns), jnp.float32),
            pltpu.SemaphoreType.DMA((2,)),
        ],
        compiler_params=pltpu.CompilerParams(vmem_limit_bytes=16 * 1024 * 1024),
    )(norms, pieces)


def solution(mesh):
    return jax.shard_map(
        functools.partial(local, mesh.shape["tile"], mesh.shape["depth"]),
        mesh=mesh,
        in_specs=(
            P(("run", "tile", "depth"), None, None),
            P(("run", "tile", "depth"), None, None),
            P(),
        ),
        out_specs=(
            P(None, ("run", "tile", "depth"), None, None),
            P(None, ("run", "tile", "depth"), None),
        ),
        check_vma=False,
    )
```

```python
import functools
import math

import jax
import jax.numpy as jnp
from jax import lax
from jax.experimental import pallas as pl
from jax.experimental.pallas import tpu as pltpu
from jax.sharding import PartitionSpec as P

MESH = pl.DeviceIdType.MESH
REACH = 3
SPREAD = 4.5
ROWS = 16
LANES = 128
BELL = [math.exp(-(k * k) / SPREAD) for k in range(-REACH, REACH + 1)]
SMOOTH = 1.0 / sum(BELL)
SLOPE = 20.0 / sum(k * k * BELL[k + REACH] for k in range(-REACH, REACH + 1))
LIGHT = (0.48, 0.6, 0.64)


def two_parts(values):
    high = values.astype(jnp.bfloat16)
    low = (values - high.astype(jnp.float32)).astype(jnp.bfloat16)
    return high, low


def plane_weights(weights_ref, depth, window, shift):
    cells = depth * ROWS
    shape = (cells, (depth + 2 * REACH) * window)
    row = lax.broadcasted_iota(jnp.int32, shape, 0)
    col = lax.broadcasted_iota(jnp.int32, shape, 1)
    dz = col // window - row // ROWS - REACH
    dx = col % window - row % ROWS - shift
    near = (jnp.abs(dz) <= REACH) & (jnp.abs(dx) <= REACH)
    dz = dz.astype(jnp.float32)
    dx = dx.astype(jnp.float32)
    bell = jnp.where(near, jnp.exp((dz * dz + dx * dx) * (-1.0 / SPREAD)), 0.0)
    parts = (
        bell * dz * (SLOPE * SMOOTH),
        bell * dx * (SLOPE * SMOOTH),
        bell * (SMOOTH * SMOOTH),
    )
    for k, part in enumerate(parts):
        high, low = two_parts(part)
        weights_ref[pl.ds(k * cells, cells), :] = high
        weights_ref[pl.ds((k + 3) * cells, cells), :] = low


def line_weights(lines_ref, columns):
    shape = (columns, columns)
    offset = lax.broadcasted_iota(jnp.int32, shape, 0) - lax.broadcasted_iota(jnp.int32, shape, 1)
    near = jnp.abs(offset) <= REACH
    offset = offset.astype(jnp.float32)
    bell = jnp.where(near, jnp.exp(offset * offset * (-1.0 / SPREAD)), 0.0)
    lines_ref[0], lines_ref[1] = two_parts(bell * SMOOTH)
    lines_ref[2], lines_ref[3] = two_parts(bell * offset * SLOPE)


def matmul(a, b):
    return jnp.dot(a, b, preferred_element_type=jnp.float32)


def lookup(table, step, position):
    lower = jnp.minimum(jnp.floor(position), table.shape[1] - 2.0)
    fraction = position - lower
    index = lower.astype(jnp.int32)
    lane = index % LANES
    group = index // LANES
    values = []
    for c in range(4):
        base = None
        for g in range(table.shape[1] // LANES):
            pair = []
            for source in (table, step):
                entries = jnp.broadcast_to(
                    source[c : c + 1, g * LANES : (g + 1) * LANES], position.shape
                )
                pair.append(
                    jnp.take_along_axis(entries, lane, axis=1, mode="promise_in_bounds")
                )
            if base is None:
                base, slope = pair
            else:
                base = jnp.where(group == g, pair[0], base)
                slope = jnp.where(group == g, pair[1], slope)
        values.append(base + fraction * slope)
    return values


def kernel(
    tiles, depths, dissolved, sorbed, table_in, norms, recv,
    cells, table_ref, weights, lines, looked, send,
    load_sem, halo_send, halo_recv, image_send, image_recv, ready,
):
    depth, rows, columns = dissolved.shape
    group = tiles * depths
    total = depth * group
    chunks = rows // ROWS
    shift = 0 if chunks == 1 else ROWS
    window = ROWS + 2 * shift
    halves = columns // LANES
    run = lax.axis_index("run")
    me = lax.axis_index("tile") * depths + lax.axis_index("depth")
    inner = pl.ds(shift, rows)

    def device(slab):
        return (run, slab // depths, slab % depths)

    def each(start, stop, body):
        lax.fori_loop(start, stop, lambda slab, carry: (body(slab), carry)[1], 0)

    barrier = pltpu.get_barrier_semaphore()

    def greet(slab):
        pl.semaphore_signal(barrier, inc=1, device_id=device(slab), device_id_type=MESH)

    def call_ready(slab):
        pl.semaphore_signal(ready, inc=1, device_id=device(slab), device_id_type=MESH)

    each(jnp.maximum(me - 1, 0), me, greet)
    each(me + 1, group, greet)

    loads = [
        pltpu.make_async_copy(dissolved, cells.at[0, pl.ds(REACH, depth), inner], load_sem.at[0]),
        pltpu.make_async_copy(table_in, table_ref, load_sem.at[1]),
        pltpu.make_async_copy(sorbed, cells.at[1, pl.ds(REACH, depth), inner], load_sem.at[2]),
    ]
    for load in loads:
        load.start()

    first, last = me == 0, me == group - 1

    @pl.when(first)
    def _():
        for field in range(2):
            cells[field, pl.ds(0, REACH), inner] = jnp.zeros((REACH, rows, columns), jnp.bfloat16)

    @pl.when(last)
    def _():
        for field in range(2):
            cells[field, pl.ds(depth + REACH, REACH), inner] = jnp.zeros(
                (REACH, rows, columns), jnp.bfloat16
            )

    if shift:
        edge = jnp.zeros((depth + 2 * REACH, shift, columns), jnp.bfloat16)
        for field in range(2):
            cells[field, :, pl.ds(0, shift)] = edge
            cells[field, :, pl.ds(shift + rows, shift)] = edge

    plane_weights(weights, depth, window, shift)

    for load in loads:
        load.wait()
    pl.semaphore_wait(barrier, jnp.minimum(me + 1, group - 1))

    def halo(field, up):
        k = 2 * field + up
        return pltpu.make_async_remote_copy(
            src_ref=cells.at[field, pl.ds(depth if up else REACH, REACH), inner],
            dst_ref=cells.at[field, pl.ds(0 if up else depth + REACH, REACH), inner],
            send_sem=halo_send.at[k],
            recv_sem=halo_recv.at[k],
            device_id=device(me + 1 if up else me - 1),
            device_id_type=MESH,
        )

    @pl.when(jnp.logical_not(last))
    def _():
        for field in range(2):
            halo(field, 1).start()

    @pl.when(jnp.logical_not(first))
    def _():
        for field in range(2):
            halo(field, 0).start()

    each(0, me - 1, call_ready)
    line_weights(lines, columns)

    table = table_ref[...]
    step = pltpu.roll(table, table.shape[1] - 1, 1) - table

    def look(x0):
        for z in range(depth):
            level = cells[0, REACH + z, pl.ds(shift + x0, ROWS), :].astype(jnp.float32)
            position = (table.shape[1] - 1.0) / (1.0 + jnp.exp(-level))
            for h in range(halves):
                span = slice(h * LANES, (h + 1) * LANES)
                for r in range(0, ROWS, 8):
                    found = lookup(table, step, position[r : r + 8, span])
                    for c in range(4):
                        looked[c, z, pl.ds(r, 8), span] = found[c]

    def shade(x0):
        plane = depth * ROWS
        flat = []
        for field in range(2):
            piece = cells[field, :, pl.ds(x0, window), :].reshape(-1, columns)
            both = matmul(weights[...], piece)
            flat.append(both[: 3 * plane] + both[3 * plane :])
        smooth_in = jnp.concatenate([flat[0][: 2 * plane], flat[1][: 2 * plane]], axis=0)
        slope_in = jnp.concatenate([flat[0][2 * plane :], flat[1][2 * plane :]], axis=0)
        high, low = two_parts(smooth_in)
        smoothed = matmul(high, lines[0]) + matmul(low, lines[0]) + matmul(high, lines[1])
        high, low = two_parts(slope_in)
        sloped = matmul(high, lines[2]) + matmul(low, lines[2]) + matmul(high, lines[3])

        emitted = [None] * 3
        transmit = None
        for z in range(depth):
            here = slice(z * ROWS, (z + 1) * ROWS)
            squares = []
            for field in range(2):
                gz = smoothed[2 * field * plane :][here]
                gx = smoothed[(2 * field + 1) * plane :][here]
                gy = sloped[field * plane :][here]
                square = gx * gx + gy * gy + gz * gz
                norms[field, z, pl.ds(x0, ROWS), :] = jnp.sqrt(square)
                squares.append(square)
                if field == 0:
                    facing = LIGHT[0] * gz + LIGHT[1] * gx + LIGHT[2] * gy
            shading = 0.25 + 0.75 * jnp.abs(facing) * lax.rsqrt(1.0 + squares[0])
            height = (me * depth + z).astype(jnp.float32)
            cue = 1.0 - (height + 0.5) * (0.5 / total)
            extinct = (3.0 / total) * looked[3, z] * (2.0 - 1.0 / (1.0 + squares[1]))
            passing = jnp.exp(-extinct)
            strength = shading * cue * (1.0 - passing)
            if z:
                strength = strength * transmit
            for c in range(3):
                colour = looked[c, z] * strength
                emitted[c] = colour if z == 0 else emitted[c] + colour
            transmit = passing if z == 0 else transmit * passing
        for c, layer in enumerate(emitted + [transmit]):
            for h in range(halves):
                send[pl.ds(x0, ROWS), c * halves + h, :] = layer[:, h * LANES : (h + 1) * LANES]

    def arrive():
        @pl.when(jnp.logical_not(first))
        def _():
            for field in range(2):
                halo(field, 1).wait_recv()

        @pl.when(jnp.logical_not(last))
        def _():
            for field in range(2):
                halo(field, 0).wait_recv()

    if chunks == 1:
        look(0)
        arrive()
        shade(0)
    else:
        arrive()

        @pl.loop(0, chunks)
        def _(chunk):
            x0 = pl.multiple_of(chunk * ROWS, ROWS)
            look(x0)
            shade(x0)

    def image(slab):
        return pltpu.make_async_remote_copy(
            src_ref=send.at[slab],
            dst_ref=recv.at[me],
            send_sem=image_send,
            recv_sem=image_recv,
            device_id=device(slab),
            device_id_type=MESH,
        )

    each(0, me, lambda slab: image(slab).start())
    each(me + 1, jnp.minimum(me + 2, group), lambda slab: image(slab).start())

    @pl.when(me < group - 2)
    def _():
        pl.semaphore_wait(ready, group - 2 - me)

    each(me + 2, group, lambda slab: image(slab).start())
    recv[me] = send[me]

    @pl.when(jnp.logical_not(last))
    def _():
        for field in range(2):
            halo(field, 1).wait_send()

    @pl.when(jnp.logical_not(first))
    def _():
        for field in range(2):
            halo(field, 0).wait_send()

    others = pltpu.make_async_remote_copy(
        src_ref=send.at[pl.ds(0, group - 1)],
        dst_ref=recv.at[pl.ds(0, group - 1)],
        send_sem=image_send,
        recv_sem=image_recv,
        device_id=device(lax.rem(me + 1, group)),
        device_id_type=MESH,
    )
    others.wait_send()
    others.wait_recv()


def finish(norms_in, pieces, norms_out, rendered_out, rendered, sem):
    group, parts, _ = pieces.shape
    halves = parts // 4
    norms_copy = pltpu.make_async_copy(norms_in, norms_out, sem.at[0])
    norms_copy.start()
    order = lax.broadcasted_iota(jnp.int32, (group, LANES), 0)
    for h in range(halves):
        span = slice(h * LANES, (h + 1) * LANES)
        through = pieces[:, 3 * halves + h, :]
        hop = 1
        while hop < group:
            through = through * jnp.where(order >= hop, pltpu.roll(through, hop, 0), 1.0)
            hop *= 2
        ahead = jnp.where(order >= 1, pltpu.roll(through, 1, 0), 1.0)
        for c in range(3):
            rendered[c, :, span] = jnp.sum(
                pieces[:, c * halves + h, :] * ahead, axis=0, keepdims=True
            )
        rendered[3, :, span] = 1.0 - through[group - 1 :]
    rendered_copy = pltpu.make_async_copy(rendered, rendered_out, sem.at[1])
    rendered_copy.start()
    norms_copy.wait()
    rendered_copy.wait()


def local(tiles, depths, dissolved, sorbed, table):
    dissolved, sorbed, table = (
        pltpu.with_memory_space_constraint(whole, pltpu.HBM) for whole in (dissolved, sorbed, table)
    )
    depth, rows, columns = dissolved.shape
    group = tiles * depths
    assert rows == group and rows % ROWS == 0 and columns % LANES == 0 and depth >= REACH
    shift = 0 if rows == ROWS else ROWS
    halves = columns // LANES
    padded = depth + 2 * REACH
    norms, pieces = pl.pallas_call(
        functools.partial(kernel, tiles, depths),
        out_shape=(
            jax.ShapeDtypeStruct((2, depth, rows, columns), jnp.float32),
            jax.ShapeDtypeStruct((group, 4 * halves, LANES), jnp.float32),
        ),
        in_specs=[pl.BlockSpec(memory_space=pltpu.HBM)] * 3,
        out_specs=(pl.BlockSpec(memory_space=pltpu.VMEM),) * 2,
        scratch_shapes=[
            pltpu.VMEM((2, padded, rows + 2 * shift, columns), jnp.bfloat16),
            pltpu.VMEM(table.shape, jnp.float32),
            pltpu.VMEM((6 * depth * ROWS, padded * (ROWS + 2 * shift)), jnp.bfloat16),
            pltpu.VMEM((4, columns, columns), jnp.bfloat16),
            pltpu.VMEM((4, depth, ROWS, columns), jnp.float32),
            pltpu.VMEM((group, 4 * halves, LANES), jnp.float32),
            pltpu.SemaphoreType.DMA((3,)),
            pltpu.SemaphoreType.DMA((4,)),
            pltpu.SemaphoreType.DMA((4,)),
            pltpu.SemaphoreType.DMA,
            pltpu.SemaphoreType.DMA,
            pltpu.SemaphoreType.REGULAR,
        ],
        compiler_params=pltpu.CompilerParams(
            collective_id=0, has_side_effects=True, vmem_limit_bytes=32 * 1024 * 1024
        ),
    )(dissolved, sorbed, table)
    return pl.pallas_call(
        finish,
        out_shape=(
            jax.ShapeDtypeStruct((2, depth, rows, columns), jnp.float32),
            jax.ShapeDtypeStruct((4, rows // group, columns), jnp.float32),
        ),
        in_specs=[pl.BlockSpec(memory_space=pltpu.VMEM)] * 2,
        out_specs=(pl.BlockSpec(memory_space=pltpu.HBM),) * 2,
        scratch_shapes=[
            pltpu.VMEM((4, rows // group, columns), jnp.float32),
            pltpu.SemaphoreType.DMA((2,)),
        ],
        compiler_params=pltpu.CompilerParams(vmem_limit_bytes=16 * 1024 * 1024),
    )(norms, pieces)


def solution(mesh):
    return jax.shard_map(
        functools.partial(local, mesh.shape["tile"], mesh.shape["depth"]),
        mesh=mesh,
        in_specs=(
            P(("run", "tile", "depth"), None, None),
            P(("run", "tile", "depth"), None, None),
            P(),
        ),
        out_specs=(
            P(None, ("run", "tile", "depth"), None, None),
            P(None, ("run", "tile", "depth"), None),
        ),
        check_vma=False,
    )
```

```python
import functools
import math

import jax
import jax.numpy as jnp
from jax import lax
from jax.experimental import pallas as pl
from jax.experimental.pallas import tpu as pltpu
from jax.sharding import PartitionSpec as P

MESH = pl.DeviceIdType.MESH
REACH = 3
SPREAD = 4.5
ROWS = 16
LANES = 128
BELL = [math.exp(-(k * k) / SPREAD) for k in range(-REACH, REACH + 1)]
SMOOTH = 1.0 / sum(BELL)
SLOPE = 20.0 / sum(k * k * BELL[k + REACH] for k in range(-REACH, REACH + 1))
LIGHT = (0.48, 0.6, 0.64)


def two_parts(values):
    high = values.astype(jnp.bfloat16)
    low = (values - high.astype(jnp.float32)).astype(jnp.bfloat16)
    return high, low


def plane_weights(weights_ref, depth, window, shift):
    cells = depth * ROWS
    shape = (cells, (depth + 2 * REACH) * window)
    row = lax.broadcasted_iota(jnp.int32, shape, 0)
    col = lax.broadcasted_iota(jnp.int32, shape, 1)
    dz = col // window - row // ROWS - REACH
    dx = col % window - row % ROWS - shift
    near = (jnp.abs(dz) <= REACH) & (jnp.abs(dx) <= REACH)
    dz = dz.astype(jnp.float32)
    dx = dx.astype(jnp.float32)
    bell = jnp.where(near, jnp.exp((dz * dz + dx * dx) * (-1.0 / SPREAD)), 0.0)
    parts = (
        bell * dz * (SLOPE * SMOOTH),
        bell * dx * (SLOPE * SMOOTH),
        bell * (SMOOTH * SMOOTH),
    )
    for k, part in enumerate(parts):
        high, low = two_parts(part)
        weights_ref[pl.ds(k * cells, cells), :] = high
        weights_ref[pl.ds((k + 3) * cells, cells), :] = low


def line_weights(lines_ref, columns):
    shape = (columns, columns)
    offset = lax.broadcasted_iota(jnp.int32, shape, 0) - lax.broadcasted_iota(jnp.int32, shape, 1)
    near = jnp.abs(offset) <= REACH
    offset = offset.astype(jnp.float32)
    bell = jnp.where(near, jnp.exp(offset * offset * (-1.0 / SPREAD)), 0.0)
    lines_ref[0], lines_ref[1] = two_parts(bell * SMOOTH)
    lines_ref[2], lines_ref[3] = two_parts(bell * offset * SLOPE)


def matmul(a, b):
    return jnp.dot(a, b, preferred_element_type=jnp.float32)


def lookup(table, step, position):
    lower = jnp.minimum(jnp.floor(position), table.shape[1] - 2.0)
    fraction = position - lower
    index = lower.astype(jnp.int32)
    lane = index % LANES
    group = index // LANES
    values = []
    for c in range(4):
        base = None
        for g in range(table.shape[1] // LANES):
            pair = []
            for source in (table, step):
                entries = jnp.broadcast_to(
                    source[c : c + 1, g * LANES : (g + 1) * LANES], position.shape
                )
                pair.append(
                    jnp.take_along_axis(entries, lane, axis=1, mode="promise_in_bounds")
                )
            if base is None:
                base, slope = pair
            else:
                base = jnp.where(group == g, pair[0], base)
                slope = jnp.where(group == g, pair[1], slope)
        values.append(base + fraction * slope)
    return values


def kernel(
    tiles, depths, dissolved, sorbed, table_in, norms, recv,
    cells, table_ref, weights, lines, looked, send,
    load_sem, halo_send, halo_recv, image_send, image_recv, ready,
):
    depth, rows, columns = dissolved.shape
    group = tiles * depths
    total = depth * group
    chunks = rows // ROWS
    shift = 0 if chunks == 1 else ROWS
    window = ROWS + 2 * shift
    halves = columns // LANES
    run = lax.axis_index("run")
    me = lax.axis_index("tile") * depths + lax.axis_index("depth")
    inner = pl.ds(shift, rows)

    def device(slab):
        return (run, slab // depths, slab % depths)

    def each(start, stop, body):
        lax.fori_loop(start, stop, lambda slab, carry: (body(slab), carry)[1], 0)

    barrier = pltpu.get_barrier_semaphore()

    def greet(slab):
        pl.semaphore_signal(barrier, inc=1, device_id=device(slab), device_id_type=MESH)

    def call_ready(slab):
        pl.semaphore_signal(ready, inc=1, device_id=device(slab), device_id_type=MESH)

    each(jnp.maximum(me - 1, 0), me, greet)
    each(me + 1, group, greet)

    loads = [
        pltpu.make_async_copy(dissolved, cells.at[0, pl.ds(REACH, depth), inner], load_sem.at[0]),
        pltpu.make_async_copy(table_in, table_ref, load_sem.at[1]),
        pltpu.make_async_copy(sorbed, cells.at[1, pl.ds(REACH, depth), inner], load_sem.at[2]),
    ]
    for load in loads:
        load.start()

    first, last = me == 0, me == group - 1

    @pl.when(first)
    def _():
        for field in range(2):
            cells[field, pl.ds(0, REACH), inner] = jnp.zeros((REACH, rows, columns), jnp.bfloat16)

    @pl.when(last)
    def _():
        for field in range(2):
            cells[field, pl.ds(depth + REACH, REACH), inner] = jnp.zeros(
                (REACH, rows, columns), jnp.bfloat16
            )

    if shift:
        edge = jnp.zeros((depth + 2 * REACH, shift, columns), jnp.bfloat16)
        for field in range(2):
            cells[field, :, pl.ds(0, shift)] = edge
            cells[field, :, pl.ds(shift + rows, shift)] = edge

    plane_weights(weights, depth, window, shift)

    for load in loads:
        load.wait()
    pl.semaphore_wait(barrier, jnp.minimum(me + 1, group - 1))

    def halo(up):
        return pltpu.make_async_remote_copy(
            src_ref=cells.at[:, pl.ds(depth if up else REACH, REACH), inner],
            dst_ref=cells.at[:, pl.ds(0 if up else depth + REACH, REACH), inner],
            send_sem=halo_send.at[up],
            recv_sem=halo_recv.at[up],
            device_id=device(me + 1 if up else me - 1),
            device_id_type=MESH,
        )

    @pl.when(jnp.logical_not(last))
    def _():
        halo(1).start()

    @pl.when(jnp.logical_not(first))
    def _():
        halo(0).start()

    each(0, me - 1, call_ready)
    line_weights(lines, columns)

    table = table_ref[...]
    step = pltpu.roll(table, table.shape[1] - 1, 1) - table

    def look(x0):
        for z in range(depth):
            level = cells[0, REACH + z, pl.ds(shift + x0, ROWS), :].astype(jnp.float32)
            position = (table.shape[1] - 1.0) / (1.0 + jnp.exp(-level))
            for h in range(halves):
                span = slice(h * LANES, (h + 1) * LANES)
                for r in range(0, ROWS, 8):
                    found = lookup(table, step, position[r : r + 8, span])
                    for c in range(4):
                        looked[c, z, pl.ds(r, 8), span] = found[c]

    def shade(x0):
        plane = depth * ROWS
        flat = []
        for field in range(2):
            piece = cells[field, :, pl.ds(x0, window), :].reshape(-1, columns)
            both = matmul(weights[...], piece)
            flat.append(both[: 3 * plane] + both[3 * plane :])
        smooth_in = jnp.concatenate([flat[0][: 2 * plane], flat[1][: 2 * plane]], axis=0)
        slope_in = jnp.concatenate([flat[0][2 * plane :], flat[1][2 * plane :]], axis=0)
        high, low = two_parts(smooth_in)
        smoothed = matmul(high, lines[0]) + matmul(low, lines[0]) + matmul(high, lines[1])
        high, low = two_parts(slope_in)
        sloped = matmul(high, lines[2]) + matmul(low, lines[2]) + matmul(high, lines[3])

        emitted = [None] * 3
        transmit = None
        for z in range(depth):
            here = slice(z * ROWS, (z + 1) * ROWS)
            squares = []
            for field in range(2):
                gz = smoothed[2 * field * plane :][here]
                gx = smoothed[(2 * field + 1) * plane :][here]
                gy = sloped[field * plane :][here]
                square = gx * gx + gy * gy + gz * gz
                norms[field, z, pl.ds(x0, ROWS), :] = jnp.sqrt(square)
                squares.append(square)
                if field == 0:
                    facing = LIGHT[0] * gz + LIGHT[1] * gx + LIGHT[2] * gy
            shading = 0.25 + 0.75 * jnp.abs(facing) * lax.rsqrt(1.0 + squares[0])
            height = (me * depth + z).astype(jnp.float32)
            cue = 1.0 - (height + 0.5) * (0.5 / total)
            extinct = (3.0 / total) * looked[3, z] * (2.0 - 1.0 / (1.0 + squares[1]))
            passing = jnp.exp(-extinct)
            strength = shading * cue * (1.0 - passing)
            if z:
                strength = strength * transmit
            for c in range(3):
                colour = looked[c, z] * strength
                emitted[c] = colour if z == 0 else emitted[c] + colour
            transmit = passing if z == 0 else transmit * passing
        for c, layer in enumerate(emitted + [transmit]):
            for h in range(halves):
                send[pl.ds(x0, ROWS), c * halves + h, :] = layer[:, h * LANES : (h + 1) * LANES]

    def arrive():
        @pl.when(jnp.logical_not(first))
        def _():
            halo(1).wait_recv()

        @pl.when(jnp.logical_not(last))
        def _():
            halo(0).wait_recv()

    if chunks == 1:
        look(0)
        arrive()
        shade(0)
    else:
        arrive()

        @pl.loop(0, chunks)
        def _(chunk):
            x0 = pl.multiple_of(chunk * ROWS, ROWS)
            look(x0)
            shade(x0)

    def image(slab):
        return pltpu.make_async_remote_copy(
            src_ref=send.at[slab],
            dst_ref=recv.at[me],
            send_sem=image_send,
            recv_sem=image_recv,
            device_id=device(slab),
            device_id_type=MESH,
        )

    each(0, me, lambda slab: image(slab).start())
    each(me + 1, jnp.minimum(me + 2, group), lambda slab: image(slab).start())

    @pl.when(me < group - 2)
    def _():
        pl.semaphore_wait(ready, group - 2 - me)

    each(me + 2, group, lambda slab: image(slab).start())
    recv[me] = send[me]

    @pl.when(jnp.logical_not(last))
    def _():
        halo(1).wait_send()

    @pl.when(jnp.logical_not(first))
    def _():
        halo(0).wait_send()

    others = pltpu.make_async_remote_copy(
        src_ref=send.at[pl.ds(0, group - 1)],
        dst_ref=recv.at[pl.ds(0, group - 1)],
        send_sem=image_send,
        recv_sem=image_recv,
        device_id=device(lax.rem(me + 1, group)),
        device_id_type=MESH,
    )
    others.wait_send()
    others.wait_recv()


def finish(norms_in, pieces, norms_out, rendered_out, rendered, sem):
    group, parts, _ = pieces.shape
    halves = parts // 4
    norms_copy = pltpu.make_async_copy(norms_in, norms_out, sem.at[0])
    norms_copy.start()
    order = lax.broadcasted_iota(jnp.int32, (group, LANES), 0)
    for h in range(halves):
        span = slice(h * LANES, (h + 1) * LANES)
        through = pieces[:, 3 * halves + h, :]
        hop = 1
        while hop < group:
            through = through * jnp.where(order >= hop, pltpu.roll(through, hop, 0), 1.0)
            hop *= 2
        ahead = jnp.where(order >= 1, pltpu.roll(through, 1, 0), 1.0)
        for c in range(3):
            rendered[c, :, span] = jnp.sum(
                pieces[:, c * halves + h, :] * ahead, axis=0, keepdims=True
            )
        rendered[3, :, span] = 1.0 - through[group - 1 :]
    rendered_copy = pltpu.make_async_copy(rendered, rendered_out, sem.at[1])
    rendered_copy.start()
    norms_copy.wait()
    rendered_copy.wait()


def local(tiles, depths, dissolved, sorbed, table):
    dissolved, sorbed, table = (
        pltpu.with_memory_space_constraint(whole, pltpu.HBM) for whole in (dissolved, sorbed, table)
    )
    depth, rows, columns = dissolved.shape
    group = tiles * depths
    assert rows == group and rows % ROWS == 0 and columns % LANES == 0 and depth >= REACH
    shift = 0 if rows == ROWS else ROWS
    halves = columns // LANES
    padded = depth + 2 * REACH
    norms, pieces = pl.pallas_call(
        functools.partial(kernel, tiles, depths),
        out_shape=(
            jax.ShapeDtypeStruct((2, depth, rows, columns), jnp.float32),
            jax.ShapeDtypeStruct((group, 4 * halves, LANES), jnp.float32),
        ),
        in_specs=[pl.BlockSpec(memory_space=pltpu.HBM)] * 3,
        out_specs=(pl.BlockSpec(memory_space=pltpu.VMEM),) * 2,
        scratch_shapes=[
            pltpu.VMEM((2, padded, rows + 2 * shift, columns), jnp.bfloat16),
            pltpu.VMEM(table.shape, jnp.float32),
            pltpu.VMEM((6 * depth * ROWS, padded * (ROWS + 2 * shift)), jnp.bfloat16),
            pltpu.VMEM((4, columns, columns), jnp.bfloat16),
            pltpu.VMEM((4, depth, ROWS, columns), jnp.float32),
            pltpu.VMEM((group, 4 * halves, LANES), jnp.float32),
            pltpu.SemaphoreType.DMA((3,)),
            pltpu.SemaphoreType.DMA((2,)),
            pltpu.SemaphoreType.DMA((2,)),
            pltpu.SemaphoreType.DMA,
            pltpu.SemaphoreType.DMA,
            pltpu.SemaphoreType.REGULAR,
        ],
        compiler_params=pltpu.CompilerParams(
            collective_id=0, has_side_effects=True, vmem_limit_bytes=32 * 1024 * 1024
        ),
    )(dissolved, sorbed, table)
    return pl.pallas_call(
        finish,
        out_shape=(
            jax.ShapeDtypeStruct((2, depth, rows, columns), jnp.float32),
            jax.ShapeDtypeStruct((4, rows // group, columns), jnp.float32),
        ),
        in_specs=[pl.BlockSpec(memory_space=pltpu.VMEM)] * 2,
        out_specs=(pl.BlockSpec(memory_space=pltpu.HBM),) * 2,
        scratch_shapes=[
            pltpu.VMEM((4, rows // group, columns), jnp.float32),
            pltpu.SemaphoreType.DMA((2,)),
        ],
        compiler_params=pltpu.CompilerParams(vmem_limit_bytes=16 * 1024 * 1024),
    )(norms, pieces)


def solution(mesh):
    return jax.shard_map(
        functools.partial(local, mesh.shape["tile"], mesh.shape["depth"]),
        mesh=mesh,
        in_specs=(
            P(("run", "tile", "depth"), None, None),
            P(("run", "tile", "depth"), None, None),
            P(),
        ),
        out_specs=(
            P(None, ("run", "tile", "depth"), None, None),
            P(None, ("run", "tile", "depth"), None),
        ),
        check_vma=False,
    )
```
